32 devices in a mesh: span: 8 (over y, x, core), chord: 4 (over z).
Axes of the slice: x: 2, y: 2, z: 4, core: 2. Of those that a mesh axis runs over, the one named last changes fastest.
Arguments:
- adj_rhs: bfloat16 [16, 16, 320, 128], P('span', 'chord'), may hold values from -6 to 6
- diag_inv: bfloat16 [16, 16, 320, 320], P('span', 'chord'), may hold values from -0.3125 to 0.3125
- face_jac: bfloat16 [16, 16, 4, 80, 320], P('span', 'chord'), may hold values from -0.15625 to 0.15625
- face_mask: int32 [16, 16, 4], P('span', 'chord'), may hold values 0 or 1
- wall_map: int32 [16, 16, 16], P('span', 'chord'), may hold values from 0 to 255
- couple: float32 [6, 5], replicated, may hold values from -3 to 3
- shell_rhs: bfloat16 [2048, 6, 128], P(('span', 'chord')), may hold values from -6 to 6
- shell_inv: float32 [2048, 6, 6], P(('span', 'chord')), may hold values from -2.5 to 2.5
Outputs:
- fluid_adjoint: bfloat16 [16, 16, 320, 128], P('span', 'chord')
- shell_adjoint: bfloat16 [2048, 6, 128], P(('span', 'chord'))
The draws below stay inside these ranges and needn't reach their ends.
All inputs are finite; a program needn't handle non-finite values. No bound on the sum of `face_mask` on one device may be relied on, other than what follows from the above.
Results may differ from the reference program's by a relative error of at most 0.0063.
Values may be sent and summed in bfloat16 or wider, within the bound.
A program may use at most 64 MiB of HBM per device.

```python
import jax
import jax.numpy as jnp
from jax import lax

NV = 5
NF = 16
SDOF = 6
ITERS = 3
ES = 2
R = 128
BLK = 320
FACE = 80
NSE = 16
NCE = 16
SHELL_COL = 256
SHELL = 2048


def set_ends(drawn, stream_key, least, largest):
    extent = drawn.shape
    place = [jax.random.randint(jax.random.fold_in(stream_key, axis), (), 0, extent[axis]) for axis in range(len(extent))]
    drawn = drawn.at[tuple(place)].set(least)
    longest = extent.index(max(extent))
    place[longest] = (place[longest] + 1) % extent[longest]
    return drawn.at[tuple(place)].set(largest)


def block_levels(stream_key, dims, cuts, smallest, largest):
    gain, own = 1.0, jax.random.fold_in(stream_key, 6)
    for position, blocks in cuts:
        draws = jnp.exp(jax.random.uniform(jax.random.fold_in(own, position), (blocks,), jnp.float32, smallest / len(cuts), largest / len(cuts)))
        gain = gain * jnp.repeat(draws, dims[position] // blocks).reshape([-1 if axis == position else 1 for axis in range(len(dims))])
    return gain


def scatter_about(rng, extent, spread, most, split=(), held_as=jnp.bfloat16):
    drawn = jax.random.normal(rng, extent, jnp.float32) * spread
    if len(split) > 0:
        drawn = block_levels(rng, extent, split, -0.22, 0.18) * drawn
    return jnp.clip(drawn, min=-most, max=most).astype(held_as)


def setup_inputs(seed: int = 0) -> dict:
    key_of = jax.random.split(jax.random.key(seed), 9)
    adj_rhs = scatter_about(key_of[0], (NSE, NCE, BLK, R), 1.0, 6.0, ((0, 8), (1, 4)))
    diag_inv = scatter_about(key_of[1], (NSE, NCE, BLK, BLK), BLK ** -0.5, 0.3125, ((0, 8), (1, 4)))
    face_jac = scatter_about(key_of[2], (NSE, NCE, 4, FACE, BLK), (4 * BLK) ** -0.5, 0.15625, ((0, 8), (1, 4)))
    face_mask = set_ends((jax.random.randint(key_of[3], (NSE, NCE, 4), 0, 4) < 3).astype(jnp.int32), jax.random.fold_in(key_of[3], 1), 0, 1)
    wall_map = set_ends(jax.random.randint(key_of[4], (NSE, NCE, NF), 0, SHELL_COL), jax.random.fold_in(key_of[4], 1), 0, SHELL_COL - 1).astype(jnp.int32)
    couple = scatter_about(key_of[5], (SDOF, NV), 0.5, 3.0, (), jnp.float32)
    shell_rhs = scatter_about(key_of[6], (SHELL, SDOF, R), 1.0, 6.0, ((0, 32),))
    shell_inv = scatter_about(key_of[7], (SHELL, SDOF, SDOF), SDOF ** -0.5, 2.5, ((0, 32),), jnp.float32)
    return {"adj_rhs": adj_rhs, "diag_inv": diag_inv, "face_jac": face_jac, "face_mask": face_mask, "wall_map": wall_map, "couple": couple, "shell_rhs": shell_rhs, "shell_inv": shell_inv}


def block_apply(mats, vectors):
    def one_row(pair):
        return jnp.einsum('bmn,bnr->bmr', pair[0].astype(jnp.float32), pair[1].astype(jnp.float32))
    return lax.map(one_row, (mats, vectors))


def face_apply(mats, vectors):
    def one_row(pair):
        return jnp.einsum('bdmn,bnr->bdmr', pair[0].astype(jnp.float32), pair[1].astype(jnp.float32))
    return lax.map(one_row, (mats, vectors))


def assemble(adj_rhs, low_span, high_span, low_chord, high_chord, wall_in):
    rows, cols, blk, width = adj_rhs.shape
    resid = adj_rhs.astype(jnp.float32).reshape(rows, cols, 4, 4, 4, NV, width)
    resid = resid.at[:, :, 0].add(-low_span.astype(jnp.float32).reshape(rows, cols, 4, 4, NV, width))
    resid = resid.at[:, :, 3].add(-high_span.astype(jnp.float32).reshape(rows, cols, 4, 4, NV, width))
    resid = resid.at[:, :, :, 0].add(-low_chord.astype(jnp.float32).reshape(rows, cols, 4, 4, NV, width))
    resid = resid.at[:, :, :, 3].add(-high_chord.astype(jnp.float32).reshape(rows, cols, 4, 4, NV, width))
    resid = resid.at[:, :, :, :, 0].add(-wall_in.reshape(rows, cols, 4, 4, NV, width))
    return resid.reshape(rows, cols, blk, width).astype(jnp.bfloat16)


def reference(adj_rhs, diag_inv, face_jac, face_mask, wall_map, couple, shell_rhs, shell_inv):
    high = lax.Precision.HIGHEST
    rows, cols, blk, width = adj_rhs.shape
    fluid = block_apply(diag_inv, adj_rhs).astype(jnp.bfloat16)
    shell = jnp.einsum('nst,ntr->nsr', shell_inv, shell_rhs.astype(jnp.float32), precision=high).astype(jnp.bfloat16)
    strip = (jnp.arange(rows, dtype=jnp.int32) // ES) * SHELL_COL
    shell_ids = (strip[:, None, None] + wall_map).reshape(-1).astype(jnp.int32)
    for step in range(1, ITERS):
        sent = face_apply(face_jac, fluid) * face_mask.astype(jnp.float32)[:, :, :, None, None]
        sent = sent.astype(jnp.bfloat16)
        zero_span = jnp.zeros_like(sent[:1, :, 0])
        zero_chord = jnp.zeros_like(sent[:, :1, 0])
        low_span = jnp.concatenate([zero_span, sent[:-1, :, 0]], 0)
        high_span = jnp.concatenate([sent[1:, :, 1], zero_span], 0)
        low_chord = jnp.concatenate([zero_chord, sent[:, :-1, 2]], 1)
        high_chord = jnp.concatenate([sent[:, 1:, 3], zero_chord], 1)
        picked = shell[shell_ids].astype(jnp.float32)
        wall_in = jnp.einsum('sv,wsr->wvr', couple, picked, precision=high)
        fluid_wall = fluid.reshape(rows, cols, 4, 4, 4, NV, width)[:, :, :, :, 0].reshape(rows * cols * NF, NV, width)
        pushed = jnp.einsum('sv,wvr->wsr', couple, fluid_wall.astype(jnp.float32), precision=high)
        shell_load = jnp.zeros((SHELL, SDOF, width), jnp.float32).at[shell_ids].add(pushed)
        resid = assemble(adj_rhs, low_span, high_span, low_chord, high_chord, wall_in)
        fluid = block_apply(diag_inv, resid).astype(jnp.bfloat16)
        shell = jnp.einsum('nst,ntr->nsr', shell_inv, shell_rhs.astype(jnp.float32) - shell_load, precision=high).astype(jnp.bfloat16)
    return fluid, shell
```

```python
import functools

import jax
import jax.numpy as jnp
import numpy as np
from jax import lax
from jax.experimental import pallas as pl
from jax.experimental.pallas import tpu as pltpu
from jax.sharding import PartitionSpec as P

NV = 5
NF = 16
SDOF = 6
ITERS = 3
FACE = 80
BLK = 320
ROUNDS = ITERS - 1


def placement():
    m = np.arange(BLK)
    i, j, k, v = m // 80, (m // 20) % 4, (m // 5) % 4, m % 5
    out = np.zeros((BLK, 3 * FACE), np.float32)
    face = i * 20 + k * 5 + v
    low, high, wall = m[j == 0], m[j == 3], m[k == 0]
    out[low, face[low]] = 1
    out[high, FACE + face[high]] = 1
    out[wall, 2 * FACE + (v * NF + 4 * i + j)[wall]] = 1
    return out


def dot(a, b):
    return jnp.dot(a, b, preferred_element_type=jnp.float32)


def kernel(
    n_span, n_chord,
    couple, mask, wall_row, inv, rhs, place, pull, adj_h, diag_h, jac_h,
    fluid_out, shell_out,
    adj, diag, jac, fluid, low_span, high_span, low_chord, high_chord, span_out, chord_out,
    wall, part_out, part_in, csh, hot, hot_t,
    in_sem, ag_send, ag_recv, rs_send, rs_recv, face_send, face_recv,
):
    rows, cols = adj.shape[0], adj.shape[1]
    nodes = rhs.shape[1]
    width = rhs.shape[2]
    bf16, f32 = jnp.bfloat16, jnp.float32
    span, chord = lax.axis_index("span"), lax.axis_index("chord")
    elements = [(a, b) for a in range(rows) for b in range(cols)]
    mesh_id = pl.DeviceIdType.MESH

    loads = {}
    for a, b in elements:
        e = a * cols + b
        loads[a, b] = [
            pltpu.make_async_copy(adj_h.at[a, b], adj.at[a, b], in_sem.at[0, e]),
            pltpu.make_async_copy(diag_h.at[a, b], diag.at[a, b], in_sem.at[1, e]),
            pltpu.make_async_copy(jac_h.at[a, b], jac.at[a, b], in_sem.at[2, e]),
        ]
        for copy in loads[a, b]:
            copy.start()

    barrier = pltpu.get_barrier_semaphore()
    for k in range(1, n_chord):
        pl.semaphore_signal(
            barrier, inc=1, device_id=(span, lax.rem(chord + k, n_chord)), device_id_type=mesh_id
        )

    @pl.when(span > 0)
    def _():
        pl.semaphore_signal(barrier, inc=1, device_id=(span - 1, chord), device_id_type=mesh_id)

    @pl.when(span < n_span - 1)
    def _():
        pl.semaphore_signal(barrier, inc=1, device_id=(span + 1, chord), device_id_type=mesh_id)

    @pl.when(span == 0)
    def _():
        low_span[:, 0] = jnp.zeros_like(low_span[:, 0])

    @pl.when(span == n_span - 1)
    def _():
        high_span[:, rows - 1] = jnp.zeros_like(high_span[:, rows - 1])

    @pl.when(chord == 0)
    def _():
        low_chord[:, 0] = jnp.zeros_like(low_chord[:, 0])

    @pl.when(chord == n_chord - 1)
    def _():
        high_chord[:, cols - 1] = jnp.zeros_like(high_chord[:, cols - 1])

    walls = rows * cols * NF
    strip = n_chord * nodes
    node = lax.broadcasted_iota(jnp.int32, (strip, walls), 0)
    h = (node == wall_row[...]).astype(f32)
    hot[...] = h.astype(bf16)
    hot_t[...] = h.T.astype(bf16)

    def coup(s, v):
        return couple[s, v]

    def shell_of(load):
        x = [rhs[t].astype(f32) for t in range(SDOF)]
        if load is not None:
            x = [x[t] - load[t] for t in range(SDOF)]
        out = []
        for s in range(SDOF):
            acc = None
            for t in range(SDOF):
                term = inv[:, SDOF * s + t : SDOF * s + t + 1] * x[t]
                acc = term if acc is None else acc + term
            out.append(acc.astype(bf16))
        return out

    def ag_copy(r, k):
        return pltpu.make_async_remote_copy(
            src_ref=csh.at[r, chord],
            dst_ref=csh.at[r, chord],
            send_sem=ag_send.at[r, k],
            recv_sem=ag_recv.at[r, k],
            device_id=(span, lax.rem(chord + k, n_chord)),
            device_id_type=mesh_id,
        )

    def ag_wait(r):
        for k in range(1, n_chord):
            src = lax.rem(chord + n_chord - k, n_chord)
            pltpu.make_async_remote_copy(
                src_ref=csh.at[r, src],
                dst_ref=csh.at[r, src],
                send_sem=ag_send.at[r, k],
                recv_sem=ag_recv.at[r, k],
                device_id=(span, src),
                device_id_type=mesh_id,
            ).wait_recv()

    def gather_shell(r, shell):
        s32 = [s.astype(f32) for s in shell]
        for v in range(NV):
            acc = None
            for s in range(SDOF):
                term = coup(s, v) * s32[s]
                acc = term if acc is None else acc + term
            csh[r, chord, :, v * width : (v + 1) * width] = acc.astype(bf16)

    def rs_copy(r, k):
        to = lax.rem(chord + k, n_chord)
        return pltpu.make_async_remote_copy(
            src_ref=part_out.at[r, to],
            dst_ref=part_in.at[r, k],
            send_sem=rs_send.at[r, k],
            recv_sem=rs_recv.at[r, k],
            device_id=(span, to),
            device_id_type=mesh_id,
        )

    def send_parts(r):
        for c in range(n_chord):
            part_out[r, c] = dot(hot[c * nodes : (c + 1) * nodes], wall[...]).astype(bf16)
        for k in range(1, n_chord):
            rs_copy(r, k).start()

    def load_of(r):
        total = part_out[r, chord].astype(f32)
        for k in range(1, n_chord):
            rs_copy(r, k).wait_recv()
            total = total + part_in[r, k].astype(f32)
        load = []
        for s in range(SDOF):
            acc = None
            for v in range(NV):
                term = coup(s, v) * total[:, v * width : (v + 1) * width]
                acc = term if acc is None else acc + term
            load.append(acc)
        return load

    def face_copy(r, d):
        src = [span_out.at[r, 0], span_out.at[r, 1], chord_out.at[r, 0], chord_out.at[r, 1]][d]
        dst = [
            low_span.at[r, 0], high_span.at[r, rows - 1],
            low_chord.at[r, 0], high_chord.at[r, cols - 1],
        ][d]
        to = [(span + 1, chord), (span - 1, chord), (span, chord + 1), (span, chord - 1)][d]
        return pltpu.make_async_remote_copy(
            src_ref=src, dst_ref=dst,
            send_sem=face_send.at[r, d], recv_sem=face_recv.at[r, d],
            device_id=to, device_id_type=mesh_id,
        )

    sends = [span < n_span - 1, span > 0, chord < n_chord - 1, chord > 0]
    gets = [span > 0, span < n_span - 1, chord > 0, chord < n_chord - 1]

    def when_do(cond, do):
        @pl.when(cond)
        def _():
            do()

    def emit_faces(r, a, b, x):
        sent = dot(jac[a, b].reshape(BLK, BLK), x)
        face = [
            (sent[d * FACE : (d + 1) * FACE] * mask[a, b, d].astype(f32)).astype(bf16)
            for d in range(4)
        ]
        if a + 1 < rows:
            low_span[r, a + 1, b] = face[0]
        else:
            span_out[r, 0, b] = face[0]
        if a > 0:
            high_span[r, a - 1, b] = face[1]
        else:
            span_out[r, 1, b] = face[1]
        if b + 1 < cols:
            low_chord[r, b + 1, a] = face[2]
        else:
            chord_out[r, 0, a] = face[2]
        if b > 0:
            high_chord[r, b - 1, a] = face[3]
        else:
            chord_out[r, 1, a] = face[3]

    def emit_wall(a, b, x):
        rim = dot(pull[...], x).astype(bf16)
        e = a * cols + b
        for v in range(NV):
            wall[e * NF : (e + 1) * NF, v * width : (v + 1) * width] = rim[v * NF : (v + 1) * NF]

    def send_faces(r):
        for d in range(4):
            when_do(sends[d], lambda d=d: face_copy(r, d).start())

    def new_fluid(r, a, b, wall_in):
        e = a * cols + b
        rim = [
            wall_in[e * NF : (e + 1) * NF, v * width : (v + 1) * width] for v in range(NV)
        ]
        moved = dot(place[...], jnp.concatenate([low_chord[r, b, a], high_chord[r, b, a]] + rim, 0))
        x = adj[a, b].astype(f32) - moved
        x = jnp.concatenate(
            [
                x[:FACE] - low_span[r, a, b].astype(f32),
                x[FACE : BLK - FACE],
                x[BLK - FACE :] - high_span[r, a, b].astype(f32),
            ],
            0,
        )
        return dot(diag[a, b], x.astype(bf16)).astype(bf16)

    shell = shell_of(None)
    gather_shell(0, shell)
    pl.semaphore_wait(
        barrier,
        n_chord - 1 + (span > 0).astype(jnp.int32) + (span < n_span - 1).astype(jnp.int32),
    )
    for k in range(1, n_chord):
        ag_copy(0, k).start()

    for a, b in elements:
        loads[a, b][0].wait()
        loads[a, b][1].wait()
        x = dot(diag[a, b], adj[a, b]).astype(bf16)
        fluid[a, b] = x
        emit_wall(a, b, x)
    send_parts(0)
    for a, b in elements:
        loads[a, b][2].wait()
        emit_faces(0, a, b, fluid[a, b])
    send_faces(0)

    for r in range(ROUNDS):
        last = r == ROUNDS - 1
        if last:
            shell = shell_of(load_of(r))
            for s in range(SDOF):
                shell_out[s] = shell[s]
        ag_wait(r)
        wall_in = dot(hot_t[...], csh[r].reshape(strip, NV * width)).astype(bf16)
        for d in range(4):
            when_do(gets[d], lambda d=d: face_copy(r, d).wait_recv())
        for a, b in elements:
            x = new_fluid(r, a, b, wall_in)
            if last:
                fluid_out[a, b] = x
            else:
                fluid[a, b] = x
                emit_wall(a, b, x)
        if not last:
            send_parts(r + 1)
            for a, b in elements:
                emit_faces(r + 1, a, b, fluid[a, b])
            send_faces(r + 1)
            shell = shell_of(load_of(r))
            gather_shell(r + 1, shell)
            for k in range(1, n_chord):
                ag_copy(r + 1, k).start()

    for r in range(ROUNDS):
        for k in range(1, n_chord):
            ag_copy(r, k).wait_send()
            rs_copy(r, k).wait_send()
        for d in range(4):
            when_do(sends[d], lambda d=d: face_copy(r, d).wait_send())


def per_device(n_span, n_chord, adj_rhs, diag_inv, face_jac, face_mask, wall_map, couple, shell_rhs, shell_inv):
    rows, cols, blk, width = adj_rhs.shape
    nodes = shell_rhs.shape[0]
    walls = rows * cols * NF
    strip = n_chord * nodes
    bf16 = jnp.bfloat16
    place = placement()
    vmem = pl.BlockSpec(memory_space=pltpu.VMEM)
    smem = pl.BlockSpec(memory_space=pltpu.SMEM)
    hbm = pl.BlockSpec(memory_space=pl.ANY)
    sem = pltpu.SemaphoreType.DMA
    fluid, shell = pl.pallas_call(
        functools.partial(kernel, n_span, n_chord),
        out_shape=(
            jax.ShapeDtypeStruct((rows, cols, blk, width), bf16),
            jax.ShapeDtypeStruct((SDOF, nodes, width), bf16),
        ),
        in_specs=[smem, smem, vmem, vmem, vmem, vmem, vmem, hbm, hbm, hbm],
        out_specs=(vmem, vmem),
        scratch_shapes=[
            pltpu.VMEM((rows, cols, blk, width), bf16),
            pltpu.VMEM((rows, cols, blk, blk), bf16),
            pltpu.VMEM((rows, cols, 4, FACE, blk), bf16),
            pltpu.VMEM((rows, cols, blk, width), bf16),
            pltpu.VMEM((ROUNDS, rows, cols, FACE, width), bf16),
            pltpu.VMEM((ROUNDS, rows, cols, FACE, width), bf16),
            pltpu.VMEM((ROUNDS, cols, rows, FACE, width), bf16),
            pltpu.VMEM((ROUNDS, cols, rows, FACE, width), bf16),
            pltpu.VMEM((ROUNDS, 2, cols, FACE, width), bf16),
            pltpu.VMEM((ROUNDS, 2, rows, FACE, width), bf16),
            pltpu.VMEM((walls, NV * width), bf16),
            pltpu.VMEM((ROUNDS, n_chord, nodes, NV * width), bf16),
            pltpu.VMEM((ROUNDS, n_chord, nodes, NV * width), bf16),
            pltpu.VMEM((ROUNDS, n_chord, nodes, NV * width), bf16),
            pltpu.VMEM((strip, walls), bf16),
            pltpu.VMEM((walls, strip), bf16),
            sem((3, rows * cols)),
            sem((ROUNDS, n_chord)),
            sem((ROUNDS, n_chord)),
            sem((ROUNDS, n_chord)),
            sem((ROUNDS, n_chord)),
            sem((ROUNDS, 4)),
            sem((ROUNDS, 4)),
        ],
        compiler_params=pltpu.CompilerParams(
            collective_id=0, has_side_effects=True, vmem_limit_bytes=48 * 2**20
        ),
    )(
        couple,
        face_mask,
        wall_map.reshape(1, walls),
        shell_inv.reshape(nodes, SDOF * SDOF),
        shell_rhs.transpose(1, 0, 2),
        jnp.asarray(place, bf16),
        jnp.asarray(place[:, 2 * FACE :].T, bf16),
        adj_rhs,
        diag_inv,
        face_jac,
    )
    return fluid, shell.transpose(1, 0, 2)


def solution(mesh):
    return jax.shard_map(
        functools.partial(per_device, mesh.shape["span"], mesh.shape["chord"]),
        mesh=mesh,
        in_specs=(
            P("span", "chord", None, None),
            P("span", "chord", None, None),
            P("span", "chord", None, None, None),
            P("span", "chord", None),
            P("span", "chord", None),
            P(),
            P(("span", "chord"), None, None),
            P(("span", "chord"), None, None),
        ),
        out_specs=(P("span", "chord", None, None), P(("span", "chord"), None, None)),
        check_vma=False,
    )
```

```python
import functools

import jax
import jax.numpy as jnp
import numpy as np
from jax import lax
from jax.experimental import pallas as pl
from jax.experimental.pallas import tpu as pltpu
from jax.sharding import PartitionSpec as P

NV = 5
NF = 16
SDOF = 6
ITERS = 3
FACE = 80
BLK = 320
ROUNDS = ITERS - 1


def placement():
    m = np.arange(BLK)
    i, j, k, v = m // 80, (m // 20) % 4, (m // 5) % 4, m % 5
    out = np.zeros((BLK, 3 * FACE), np.float32)
    face = i * 20 + k * 5 + v
    low, high, wall = m[j == 0], m[j == 3], m[k == 0]
    out[low, face[low]] = 1
    out[high, FACE + face[high]] = 1
    out[wall, 2 * FACE + (v * NF + 4 * i + j)[wall]] = 1
    return out


def dot(a, b):
    return jnp.dot(a, b, preferred_element_type=jnp.float32)


def kernel(
    n_span, n_chord,
    couple, mask, wall_map, inv_t, rhs_h, place_h, pull_h, adj_h, diag_h, jac_h,
    fluid_out, shell_out,
    rhs, place, pull, adj, diag, jac, fluid, low_span, high_span, low_chord, high_chord, span_out, chord_out,
    wall, own, part_out, part_in, csh, hot, hot_t,
    small_sem, in_sem, ag_send, ag_recv, rs_send, rs_recv, face_send, face_recv,
):
    rows, cols = adj.shape[0], adj.shape[1]
    nodes = rhs.shape[1]
    width = rhs.shape[2]
    bf16, f32 = jnp.bfloat16, jnp.float32
    span, chord = lax.axis_index("span"), lax.axis_index("chord")
    elements = [(a, b) for a in range(rows) for b in range(cols)]
    mesh_id = pl.DeviceIdType.MESH

    small = [
        pltpu.make_async_copy(src, dst, small_sem.at[i])
        for i, (src, dst) in enumerate([(rhs_h, rhs), (pull_h, pull), (place_h, place)])
    ]
    loads = {}
    for a, b in elements:
        e = a * cols + b
        loads[a, b] = [
            pltpu.make_async_copy(adj_h.at[a, b], adj.at[a, b], in_sem.at[0, e]),
            pltpu.make_async_copy(diag_h.at[a, b], diag.at[a, b], in_sem.at[1, e]),
            pltpu.make_async_copy(jac_h.at[a, b], jac.at[a, b], in_sem.at[2, e]),
        ]
    small[0].start()
    small[1].start()
    for a, b in elements:
        loads[a, b][0].start()
        loads[a, b][1].start()
    for a, b in elements:
        loads[a, b][2].start()
    small[2].start()

    barrier = pltpu.get_barrier_semaphore()

    @pl.when(chord > 0)
    def _():
        pl.semaphore_signal(barrier, inc=1, device_id=(span, chord - 1), device_id_type=mesh_id)

    @pl.when(chord < n_chord - 1)
    def _():
        pl.semaphore_signal(barrier, inc=1, device_id=(span, chord + 1), device_id_type=mesh_id)

    @pl.when(span > 0)
    def _():
        pl.semaphore_signal(barrier, inc=1, device_id=(span - 1, chord), device_id_type=mesh_id)

    @pl.when(span < n_span - 1)
    def _():
        pl.semaphore_signal(barrier, inc=1, device_id=(span + 1, chord), device_id_type=mesh_id)

    @pl.when(span == 0)
    def _():
        low_span[:, 0] = jnp.zeros_like(low_span[:, 0])

    @pl.when(span == n_span - 1)
    def _():
        high_span[:, rows - 1] = jnp.zeros_like(high_span[:, rows - 1])

    @pl.when(chord == 0)
    def _():
        low_chord[:, 0] = jnp.zeros_like(low_chord[:, 0])

    @pl.when(chord == n_chord - 1)
    def _():
        high_chord[:, cols - 1] = jnp.zeros_like(high_chord[:, cols - 1])

    walls = rows * cols * NF
    strip = n_chord * nodes
    node = lax.broadcasted_iota(jnp.int32, (strip, walls), 0)
    ids = jnp.concatenate([wall_map[a] for a in range(rows)], 0)
    lane = lax.broadcasted_iota(jnp.int32, (NF, walls), 1)
    spread = (lax.broadcasted_iota(jnp.int32, (NF, walls), 0) == lane % NF).astype(bf16)
    coarse = lax.shift_right_logical(ids, 3)
    fine = ids - 8 * coarse
    tiled = 8.0 * dot(coarse.astype(f32).astype(bf16), spread) + dot(fine.astype(f32).astype(bf16), spread)
    element = lax.broadcasted_iota(jnp.int32, (rows * cols, walls), 0)
    lane = lax.broadcasted_iota(jnp.int32, (rows * cols, walls), 1)
    wall_row = jnp.sum(
        jnp.where(lax.shift_right_logical(lane, 4) == element, tiled, 0.0), axis=0, keepdims=True
    ).astype(jnp.int32)
    h = (node == wall_row).astype(f32)
    hot[...] = h.astype(bf16)
    hot_t[...] = h.T.astype(bf16)

    inv = jnp.concatenate(
        [
            jnp.concatenate([inv_t[s], jnp.zeros((8 - SDOF, nodes), f32)], 0)
            for s in range(SDOF)
        ],
        0,
    ).T

    def coup(s, v):
        return couple[s, v]

    def shell_of(load):
        x = [rhs[t].astype(f32) for t in range(SDOF)]
        if load is not None:
            x = [x[t] - load[t] for t in range(SDOF)]
        out = []
        for s in range(SDOF):
            acc = None
            for t in range(SDOF):
                term = inv[:, 8 * s + t : 8 * s + t + 1] * x[t]
                acc = term if acc is None else acc + term
            out.append(acc.astype(bf16))
        return out

    def when_do(cond, do):
        @pl.when(cond)
        def _():
            do()

    has_low, has_high = chord > 0, chord < n_chord - 1

    def ag_copy(r, way, s, block):
        to = (span, chord + 1) if way == 0 else (span, chord - 1)
        return pltpu.make_async_remote_copy(
            src_ref=csh.at[r, block],
            dst_ref=csh.at[r, block],
            send_sem=ag_send.at[r, way, s],
            recv_sem=ag_recv.at[r, way, s],
            device_id=to,
            device_id_type=mesh_id,
        )

    def ag_held(s):
        return chord - s, chord + s, chord >= s, chord + s < n_chord

    def ag_start(r):
        when_do(has_high, lambda: ag_copy(r, 0, 0, chord).start())
        when_do(has_low, lambda: ag_copy(r, 1, 0, chord).start())

    def ag_relay(r, s):
        up, down, up_ok, down_ok = ag_held(s)

        @pl.when(up_ok)
        def _():
            ag_copy(r, 0, s - 1, up).wait_recv()
            if s < n_chord - 1:
                when_do(has_high, lambda: ag_copy(r, 0, s, up).start())

        @pl.when(down_ok)
        def _():
            ag_copy(r, 1, s - 1, down).wait_recv()
            if s < n_chord - 1:
                when_do(has_low, lambda: ag_copy(r, 1, s, down).start())

    def ag_sent(r):
        for s in range(n_chord - 1):
            up, down, up_ok, down_ok = ag_held(s)
            when_do(up_ok & has_high, lambda: ag_copy(r, 0, s, up).wait_send())
            when_do(down_ok & has_low, lambda: ag_copy(r, 1, s, down).wait_send())

    def gather_shell(r, shell):
        s32 = [s.astype(f32) for s in shell]
        for v in range(NV):
            acc = None
            for s in range(SDOF):
                term = coup(s, v) * s32[s]
                acc = term if acc is None else acc + term
            csh[r, chord, :, v * width : (v + 1) * width] = acc.astype(bf16)

    def rs_copy(r, way, k):
        return pltpu.make_async_remote_copy(
            src_ref=part_out.at[r, way, k],
            dst_ref=part_in.at[r, way, k],
            send_sem=rs_send.at[r, way, k],
            recv_sem=rs_recv.at[r, way, k],
            device_id=(span, chord + 1) if way == 0 else (span, chord - 1),
            device_id_type=mesh_id,
        )

    def rs_start(r):
        for c in range(n_chord):
            own[r, c] = dot(hot[c * nodes : (c + 1) * nodes], wall[...])
        for k in range(n_chord - 1, 0, -1):

            @pl.when(chord == 0)
            def _():
                part_out[r, 0, k] = own[r, k].astype(bf16)
                rs_copy(r, 0, k).start()

            @pl.when(chord == n_chord - 1)
            def _():
                part_out[r, 1, k] = own[r, n_chord - 1 - k].astype(bf16)
                rs_copy(r, 1, k).start()

    def rs_relay(r, k):
        @pl.when((chord > 0) & (chord + k < n_chord))
        def _():
            rs_copy(r, 0, k + 1).wait_recv()
            part_out[r, 0, k] = (own[r, chord + k] + part_in[r, 0, k + 1].astype(f32)).astype(bf16)
            rs_copy(r, 0, k).start()

        @pl.when((chord < n_chord - 1) & (chord >= k))
        def _():
            rs_copy(r, 1, k + 1).wait_recv()
            part_out[r, 1, k] = (own[r, chord - k] + part_in[r, 1, k + 1].astype(f32)).astype(bf16)
            rs_copy(r, 1, k).start()

    def rs_sent(r):
        for k in range(1, n_chord):
            when_do(chord + k < n_chord, lambda: rs_copy(r, 0, k).wait_send())
            when_do(chord >= k, lambda: rs_copy(r, 1, k).wait_send())

    def load_of(r):
        @pl.when(has_low)
        def _():
            rs_copy(r, 0, 1).wait_recv()
            own[r, chord] = own[r, chord] + part_in[r, 0, 1].astype(f32)

        @pl.when(has_high)
        def _():
            rs_copy(r, 1, 1).wait_recv()
            own[r, chord] = own[r, chord] + part_in[r, 1, 1].astype(f32)

        total = own[r, chord]
        load = []
        for s in range(SDOF):
            acc = None
            for v in range(NV):
                term = coup(s, v) * total[:, v * width : (v + 1) * width]
                acc = term if acc is None else acc + term
            load.append(acc)
        return load

    def face_copy(r, d):
        src = [span_out.at[r, 0], span_out.at[r, 1], chord_out.at[r, 0], chord_out.at[r, 1]][d]
        dst = [
            low_span.at[r, 0], high_span.at[r, rows - 1],
            low_chord.at[r, 0], high_chord.at[r, cols - 1],
        ][d]
        to = [(span + 1, chord), (span - 1, chord), (span, chord + 1), (span, chord - 1)][d]
        return pltpu.make_async_remote_copy(
            src_ref=src, dst_ref=dst,
            send_sem=face_send.at[r, d], recv_sem=face_recv.at[r, d],
            device_id=to, device_id_type=mesh_id,
        )

    sends = [span < n_span - 1, span > 0, chord < n_chord - 1, chord > 0]
    gets = [span > 0, span < n_span - 1, chord > 0, chord < n_chord - 1]

    def emit_faces(r, a, b, x):
        sent = dot(jac[a, b].reshape(BLK, BLK), x)
        face = [
            (sent[d * FACE : (d + 1) * FACE] * mask[a, b, d].astype(f32)).astype(bf16)
            for d in range(4)
        ]
        if a + 1 < rows:
            low_span[r, a + 1, b] = face[0]
        else:
            span_out[r, 0, b] = face[0]
        if a > 0:
            high_span[r, a - 1, b] = face[1]
        else:
            span_out[r, 1, b] = face[1]
        if b + 1 < cols:
            low_chord[r, b + 1, a] = face[2]
        else:
            chord_out[r, 0, a] = face[2]
        if b > 0:
            high_chord[r, b - 1, a] = face[3]
        else:
            chord_out[r, 1, a] = face[3]

    def emit_wall(a, b, x):
        rim = dot(pull[...], x).astype(bf16)
        e = a * cols + b
        for v in range(NV):
            wall[e * NF : (e + 1) * NF, v * width : (v + 1) * width] = rim[v * NF : (v + 1) * NF]

    def send_faces(r):
        for d in range(4):
            when_do(sends[d], lambda d=d: face_copy(r, d).start())

    def new_fluid(r, a, b, wall_in):
        e = a * cols + b
        rim = [
            wall_in[e * NF : (e + 1) * NF, v * width : (v + 1) * width] for v in range(NV)
        ]
        moved = dot(place[...], jnp.concatenate([low_chord[r, b, a], high_chord[r, b, a]] + rim, 0))
        x = adj[a, b].astype(f32) - moved
        x = jnp.concatenate(
            [
                x[:FACE] - low_span[r, a, b].astype(f32),
                x[FACE : BLK - FACE],
                x[BLK - FACE :] - high_span[r, a, b].astype(f32),
            ],
            0,
        )
        return dot(diag[a, b], x.astype(bf16)).astype(bf16)

    def faces_sent(r):
        for d in range(4):
            when_do(sends[d], lambda d=d: face_copy(r, d).wait_send())

    small[0].wait()
    gather_shell(0, shell_of(None))
    greeted = [span > 0, span < n_span - 1, has_low, has_high]
    pl.semaphore_wait(barrier, sum(c.astype(jnp.int32) for c in greeted))
    ag_start(0)

    relays = list(range(n_chord - 2, 0, -1))
    half = (len(relays) + 1) // 2
    hops = list(range(1, n_chord))

    small[1].wait()
    count = len(elements)
    for e, (a, b) in enumerate(elements):
        loads[a, b][0].wait()
        loads[a, b][1].wait()
        x = dot(diag[a, b], adj[a, b]).astype(bf16)
        fluid[a, b] = x
        emit_wall(a, b, x)
    rs_start(0)
    ag_relay(0, hops[0])
    for e, (a, b) in enumerate(elements):
        loads[a, b][2].wait()
        emit_faces(0, a, b, fluid[a, b])
        if e == count // 2 - 1 and len(hops) > 1:
            ag_relay(0, hops[1])
    send_faces(0)
    small[2].wait()

    for r in range(ROUNDS):
        last = r == ROUNDS - 1
        if r > 0:
            for i in range(max(len(hops), len(relays))):
                if i < len(relays):
                    rs_relay(r, relays[i])
                if i < len(hops):
                    ag_relay(r, hops[i])
        else:
            for k in relays[:half]:
                rs_relay(r, k)
            for s in hops[2:]:
                ag_relay(r, s)
        wall_in = dot(hot_t[...], csh[r].reshape(strip, NV * width)).astype(bf16)
        for d in range(4):
            when_do(gets[d], lambda d=d: face_copy(r, d).wait_recv())
        for e, (a, b) in enumerate(elements):
            x = new_fluid(r, a, b, wall_in)
            if last:
                fluid_out[a, b] = x
            else:
                fluid[a, b] = x
                emit_wall(a, b, x)
            if r == 0 and e == 1:
                for k in relays[half:]:
                    rs_relay(r, k)
            if e == 5:
                shell = shell_of(load_of(r))
                if last:
                    for s in range(SDOF):
                        shell_out[s] = shell[s]
                else:
                    gather_shell(r + 1, shell)
                    ag_start(r + 1)
        if not last:
            rs_start(r + 1)
            for a, b in elements:
                emit_faces(r + 1, a, b, fluid[a, b])
            send_faces(r + 1)

    for r in range(ROUNDS):
        ag_sent(r)
        rs_sent(r)
        faces_sent(r)


def per_device(n_span, n_chord, adj_rhs, diag_inv, face_jac, face_mask, wall_map, couple, shell_rhs, shell_inv):
    rows, cols, blk, width = adj_rhs.shape
    nodes = shell_rhs.shape[0]
    walls = rows * cols * NF
    strip = n_chord * nodes
    bf16 = jnp.bfloat16
    place = placement()
    vmem = pl.BlockSpec(memory_space=pltpu.VMEM)
    smem = pl.BlockSpec(memory_space=pltpu.SMEM)
    hbm = pl.BlockSpec(memory_space=pl.ANY)
    sem = pltpu.SemaphoreType.DMA
    fluid, shell = pl.pallas_call(
        functools.partial(kernel, n_span, n_chord),
        out_shape=(
            jax.ShapeDtypeStruct((rows, cols, blk, width), bf16),
            jax.ShapeDtypeStruct((SDOF, nodes, width), bf16),
        ),
        in_specs=[smem, smem, vmem, vmem, hbm, hbm, hbm, hbm, hbm, hbm],
        out_specs=(vmem, vmem),
        scratch_shapes=[
            pltpu.VMEM((SDOF, nodes, width), bf16),
            pltpu.VMEM((blk, 3 * FACE), bf16),
            pltpu.VMEM((FACE, blk), bf16),
            pltpu.VMEM((rows, cols, blk, width), bf16),
            pltpu.VMEM((rows, cols, blk, blk), bf16),
            pltpu.VMEM((rows, cols, 4, FACE, blk), bf16),
            pltpu.VMEM((rows, cols, blk, width), bf16),
            pltpu.VMEM((ROUNDS, rows, cols, FACE, width), bf16),
            pltpu.VMEM((ROUNDS, rows, cols, FACE, width), bf16),
            pltpu.VMEM((ROUNDS, cols, rows, FACE, width), bf16),
            pltpu.VMEM((ROUNDS, cols, rows, FACE, width), bf16),
            pltpu.VMEM((ROUNDS, 2, cols, FACE, width), bf16),
            pltpu.VMEM((ROUNDS, 2, rows, FACE, width), bf16),
            pltpu.VMEM((walls, NV * width), bf16),
            pltpu.VMEM((ROUNDS, n_chord, nodes, NV * width), jnp.float32),
            pltpu.VMEM((ROUNDS, 2, n_chord, nodes, NV * width), bf16),
            pltpu.VMEM((ROUNDS, 2, n_chord, nodes, NV * width), bf16),
            pltpu.VMEM((ROUNDS, n_chord, nodes, NV * width), bf16),
            pltpu.VMEM((strip, walls), bf16),
            pltpu.VMEM((walls, strip), bf16),
            sem((3,)),
            sem((3, rows * cols)),
            sem((ROUNDS, 2, n_chord)),
            sem((ROUNDS, 2, n_chord)),
            sem((ROUNDS, 2, n_chord)),
            sem((ROUNDS, 2, n_chord)),
            sem((ROUNDS, 4)),
            sem((ROUNDS, 4)),
        ],
        compiler_params=pltpu.CompilerParams(
            collective_id=0, has_side_effects=True, vmem_limit_bytes=60 * 2**20
        ),
    )(
        couple,
        face_mask,
        wall_map,
        shell_inv.transpose(1, 2, 0),
        shell_rhs.transpose(1, 0, 2),
        jnp.asarray(place, bf16),
        jnp.asarray(place[:, 2 * FACE :].T, bf16),
        adj_rhs,
        diag_inv,
        face_jac,
    )
    return fluid, shell.transpose(1, 0, 2)


def solution(mesh):
    return jax.shard_map(
        functools.partial(per_device, mesh.shape["span"], mesh.shape["chord"]),
        mesh=mesh,
        in_specs=(
            P("span", "chord", None, None),
            P("span", "chord", None, None),
            P("span", "chord", None, None, None),
            P("span", "chord", None),
            P("span", "chord", None),
            P(),
            P(("span", "chord"), None, None),
            P(("span", "chord"), None, None),
        ),
        out_specs=(P("span", "chord", None, None), P(("span", "chord"), None, None)),
        check_vma=False,
    )
```

```python
import functools

import jax
import jax.numpy as jnp
import numpy as np
from jax import lax
from jax.experimental import pallas as pl
from jax.experimental.pallas import tpu as pltpu
from jax.sharding import PartitionSpec as P

NV = 5
NF = 16
SDOF = 6
ITERS = 3
FACE = 80
BLK = 320
ROUNDS = ITERS - 1


def placement():
    m = np.arange(BLK)
    i, j, k, v = m // 80, (m // 20) % 4, (m // 5) % 4, m % 5
    out = np.zeros((BLK, 3 * FACE), np.float32)
    face = i * 20 + k * 5 + v
    low, high, wall = m[j == 0], m[j == 3], m[k == 0]
    out[low, face[low]] = 1
    out[high, FACE + face[high]] = 1
    out[wall, 2 * FACE + (v * NF + 4 * i + j)[wall]] = 1
    return out


def dot(a, b):
    return jnp.dot(a, b, preferred_element_type=jnp.float32)


def kernel(
    n_span, n_chord,
    couple, mask, wall_map, inv_t, rhs_h, place_h, pull_h, adj_h, diag_h, jac_h,
    fluid_out, shell_out,
    rhs, place, pull, adj, diag, jac, fluid, low_span, high_span, low_chord, high_chord, span_out, chord_out,
    wall, own, part_out, part_in, csh, hot, hot_t,
    small_sem, in_sem, ag_send, ag_recv, rs_send, rs_recv, face_send, face_recv,
):
    rows, cols = adj.shape[0], adj.shape[1]
    nodes = rhs.shape[1]
    width = rhs.shape[2]
    bf16, f32 = jnp.bfloat16, jnp.float32
    span, chord = lax.axis_index("span"), lax.axis_index("chord")
    elements = [(a, b) for a in range(rows) for b in range(cols)]
    mesh_id = pl.DeviceIdType.MESH

    small = [
        pltpu.make_async_copy(src, dst, small_sem.at[i])
        for i, (src, dst) in enumerate([(rhs_h, rhs), (pull_h, pull), (place_h, place)])
    ]
    loads = {}
    for a, b in elements:
        e = a * cols + b
        loads[a, b] = [
            pltpu.make_async_copy(adj_h.at[a, b], adj.at[a, b], in_sem.at[0, e]),
            pltpu.make_async_copy(diag_h.at[a, b], diag.at[a, b], in_sem.at[1, e]),
            pltpu.make_async_copy(jac_h.at[a, b], jac.at[a, b], in_sem.at[2, e]),
        ]
    small[0].start()
    small[1].start()
    for a, b in elements:
        loads[a, b][0].start()
        loads[a, b][1].start()
    for a, b in elements:
        loads[a, b][2].start()
    small[2].start()

    barrier = pltpu.get_barrier_semaphore()

    @pl.when(chord > 0)
    def _():
        pl.semaphore_signal(barrier, inc=1, device_id=(span, chord - 1), device_id_type=mesh_id)

    @pl.when(chord < n_chord - 1)
    def _():
        pl.semaphore_signal(barrier, inc=1, device_id=(span, chord + 1), device_id_type=mesh_id)

    @pl.when(span > 0)
    def _():
        pl.semaphore_signal(barrier, inc=1, device_id=(span - 1, chord), device_id_type=mesh_id)

    @pl.when(span < n_span - 1)
    def _():
        pl.semaphore_signal(barrier, inc=1, device_id=(span + 1, chord), device_id_type=mesh_id)

    @pl.when(span == 0)
    def _():
        low_span[:, 0] = jnp.zeros_like(low_span[:, 0])

    @pl.when(span == n_span - 1)
    def _():
        high_span[:, rows - 1] = jnp.zeros_like(high_span[:, rows - 1])

    @pl.when(chord == 0)
    def _():
        low_chord[:, 0] = jnp.zeros_like(low_chord[:, 0])

    @pl.when(chord == n_chord - 1)
    def _():
        high_chord[:, cols - 1] = jnp.zeros_like(high_chord[:, cols - 1])

    walls = rows * cols * NF
    strip = n_chord * nodes
    node = lax.broadcasted_iota(jnp.int32, (strip, walls), 0)
    ids = jnp.concatenate([wall_map[a] for a in range(rows)], 0)
    lane = lax.broadcasted_iota(jnp.int32, (NF, walls), 1)
    spread = (lax.broadcasted_iota(jnp.int32, (NF, walls), 0) == lane % NF).astype(bf16)
    coarse = lax.shift_right_logical(ids, 3)
    fine = ids - 8 * coarse
    tiled = 8.0 * dot(coarse.astype(f32).astype(bf16), spread) + dot(fine.astype(f32).astype(bf16), spread)
    element = lax.broadcasted_iota(jnp.int32, (rows * cols, walls), 0)
    lane = lax.broadcasted_iota(jnp.int32, (rows * cols, walls), 1)
    wall_row = jnp.sum(
        jnp.where(lax.shift_right_logical(lane, 4) == element, tiled, 0.0), axis=0, keepdims=True
    ).astype(jnp.int32)
    h = (node == wall_row).astype(f32)
    hot[...] = h.astype(bf16)
    hot_t[...] = h.T.astype(bf16)

    inv = jnp.concatenate(
        [
            jnp.concatenate([inv_t[s], jnp.zeros((8 - SDOF, nodes), f32)], 0)
            for s in range(SDOF)
        ],
        0,
    ).T

    def coup(s, v):
        return couple[s, v]

    def shell_of(load):
        x = [rhs[t].astype(f32) for t in range(SDOF)]
        if load is not None:
            x = [x[t] - load[t] for t in range(SDOF)]
        out = []
        for s in range(SDOF):
            acc = None
            for t in range(SDOF):
                term = inv[:, 8 * s + t : 8 * s + t + 1] * x[t]
                acc = term if acc is None else acc + term
            out.append(acc.astype(bf16))
        return out

    def when_do(cond, do):
        @pl.when(cond)
        def _():
            do()

    has_low, has_high = chord > 0, chord < n_chord - 1

    def ag_copy(r, way, s, block):
        to = (span, chord + 1) if way == 0 else (span, chord - 1)
        return pltpu.make_async_remote_copy(
            src_ref=csh.at[r, block],
            dst_ref=csh.at[r, block],
            send_sem=ag_send.at[r, way, s],
            recv_sem=ag_recv.at[r, way, s],
            device_id=to,
            device_id_type=mesh_id,
        )

    def ag_held(s):
        return chord - s, chord + s, chord >= s, chord + s < n_chord

    def ag_start(r):
        when_do(has_high, lambda: ag_copy(r, 0, 0, chord).start())
        when_do(has_low, lambda: ag_copy(r, 1, 0, chord).start())

    def ag_relay(r, s):
        up, down, up_ok, down_ok = ag_held(s)

        @pl.when(up_ok)
        def _():
            ag_copy(r, 0, s - 1, up).wait_recv()
            if s < n_chord - 1:
                when_do(has_high, lambda: ag_copy(r, 0, s, up).start())

        @pl.when(down_ok)
        def _():
            ag_copy(r, 1, s - 1, down).wait_recv()
            if s < n_chord - 1:
                when_do(has_low, lambda: ag_copy(r, 1, s, down).start())

    def ag_sent(r):
        for s in range(n_chord - 1):
            up, down, up_ok, down_ok = ag_held(s)
            when_do(up_ok & has_high, lambda: ag_copy(r, 0, s, up).wait_send())
            when_do(down_ok & has_low, lambda: ag_copy(r, 1, s, down).wait_send())

    def gather_shell(r, shell):
        s32 = [s.astype(f32) for s in shell]
        for v in range(NV):
            acc = None
            for s in range(SDOF):
                term = coup(s, v) * s32[s]
                acc = term if acc is None else acc + term
            csh[r, chord, :, v * width : (v + 1) * width] = acc.astype(bf16)

    def rs_copy(r, way, k):
        return pltpu.make_async_remote_copy(
            src_ref=part_out.at[r, way, k],
            dst_ref=part_in.at[r, way, k],
            send_sem=rs_send.at[r, way, k],
            recv_sem=rs_recv.at[r, way, k],
            device_id=(span, chord + 1) if way == 0 else (span, chord - 1),
            device_id_type=mesh_id,
        )

    def rs_start(r):
        for c in range(n_chord):
            own[r, c] = dot(hot[c * nodes : (c + 1) * nodes], wall[...])
        rs_end(r, n_chord - 1)

    def rs_end(r, k):
        @pl.when(chord == 0)
        def _():
            if k < n_chord - 1:
                rs_copy(r, 0, k + 1).wait_send()
            part_out[r, 0, k] = own[r, k].astype(bf16)
            rs_copy(r, 0, k).start()

        @pl.when(chord == n_chord - 1)
        def _():
            if k < n_chord - 1:
                rs_copy(r, 1, k + 1).wait_send()
            part_out[r, 1, k] = own[r, n_chord - 1 - k].astype(bf16)
            rs_copy(r, 1, k).start()

    def rs_relay(r, k):
        rs_end(r, k)

        @pl.when((chord > 0) & (chord + k < n_chord))
        def _():
            rs_copy(r, 0, k + 1).wait_recv()
            part_out[r, 0, k] = (own[r, chord + k] + part_in[r, 0, k + 1].astype(f32)).astype(bf16)
            rs_copy(r, 0, k).start()

        @pl.when((chord < n_chord - 1) & (chord >= k))
        def _():
            rs_copy(r, 1, k + 1).wait_recv()
            part_out[r, 1, k] = (own[r, chord - k] + part_in[r, 1, k + 1].astype(f32)).astype(bf16)
            rs_copy(r, 1, k).start()

    def rs_sent(r):
        for k in range(1, n_chord):
            up, down = chord + k < n_chord, chord >= k
            if k > 1:
                up, down = up & has_low, down & has_high
            when_do(up, lambda: rs_copy(r, 0, k).wait_send())
            when_do(down, lambda: rs_copy(r, 1, k).wait_send())

    def load_of(r):
        @pl.when(has_low)
        def _():
            rs_copy(r, 0, 1).wait_recv()
            own[r, chord] = own[r, chord] + part_in[r, 0, 1].astype(f32)

        @pl.when(has_high)
        def _():
            rs_copy(r, 1, 1).wait_recv()
            own[r, chord] = own[r, chord] + part_in[r, 1, 1].astype(f32)

        total = own[r, chord]
        load = []
        for s in range(SDOF):
            acc = None
            for v in range(NV):
                term = coup(s, v) * total[:, v * width : (v + 1) * width]
                acc = term if acc is None else acc + term
            load.append(acc)
        return load

    def face_copy(r, d):
        src = [span_out.at[r, 0], span_out.at[r, 1], chord_out.at[r, 0], chord_out.at[r, 1]][d]
        dst = [
            low_span.at[r, 0], high_span.at[r, rows - 1],
            low_chord.at[r, 0], high_chord.at[r, cols - 1],
        ][d]
        to = [(span + 1, chord), (span - 1, chord), (span, chord + 1), (span, chord - 1)][d]
        return pltpu.make_async_remote_copy(
            src_ref=src, dst_ref=dst,
            send_sem=face_send.at[r, d], recv_sem=face_recv.at[r, d],
            device_id=to, device_id_type=mesh_id,
        )

    sends = [span < n_span - 1, span > 0, chord < n_chord - 1, chord > 0]
    gets = [span > 0, span < n_span - 1, chord > 0, chord < n_chord - 1]

    def emit_faces(r, a, b, x):
        sent = dot(jac[a, b].reshape(BLK, BLK), x)
        face = [
            (sent[d * FACE : (d + 1) * FACE] * mask[a, b, d].astype(f32)).astype(bf16)
            for d in range(4)
        ]
        if a + 1 < rows:
            low_span[r, a + 1, b] = face[0]
        else:
            span_out[r, 0, b] = face[0]
        if a > 0:
            high_span[r, a - 1, b] = face[1]
        else:
            span_out[r, 1, b] = face[1]
        if b + 1 < cols:
            low_chord[r, b + 1, a] = face[2]
        else:
            chord_out[r, 0, a] = face[2]
        if b > 0:
            high_chord[r, b - 1, a] = face[3]
        else:
            chord_out[r, 1, a] = face[3]

    def emit_wall(a, b, x):
        rim = dot(pull[...], x).astype(bf16)
        e = a * cols + b
        for v in range(NV):
            wall[e * NF : (e + 1) * NF, v * width : (v + 1) * width] = rim[v * NF : (v + 1) * NF]

    def send_faces(r):
        for d in range(4):
            when_do(sends[d], lambda d=d: face_copy(r, d).start())

    def new_fluid(r, a, b, wall_in):
        e = a * cols + b
        rim = [
            wall_in[e * NF : (e + 1) * NF, v * width : (v + 1) * width] for v in range(NV)
        ]
        moved = dot(place[...], jnp.concatenate([low_chord[r, b, a], high_chord[r, b, a]] + rim, 0))
        x = adj[a, b].astype(f32) - moved
        x = jnp.concatenate(
            [
                x[:FACE] - low_span[r, a, b].astype(f32),
                x[FACE : BLK - FACE],
                x[BLK - FACE :] - high_span[r, a, b].astype(f32),
            ],
            0,
        )
        return dot(diag[a, b], x.astype(bf16)).astype(bf16)

    def faces_sent(r):
        for d in range(4):
            when_do(sends[d], lambda d=d: face_copy(r, d).wait_send())

    small[0].wait()
    gather_shell(0, shell_of(None))
    greeted = [span > 0, span < n_span - 1, has_low, has_high]
    pl.semaphore_wait(barrier, sum(c.astype(jnp.int32) for c in greeted))
    ag_start(0)

    relays = list(range(n_chord - 2, 0, -1))
    half = (len(relays) + 1) // 2
    hops = list(range(1, n_chord))

    small[1].wait()
    count = len(elements)
    for e, (a, b) in enumerate(elements):
        loads[a, b][0].wait()
        loads[a, b][1].wait()
        x = dot(diag[a, b], adj[a, b]).astype(bf16)
        fluid[a, b] = x
        emit_wall(a, b, x)
    rs_start(0)
    ag_relay(0, hops[0])
    for e, (a, b) in enumerate(elements):
        loads[a, b][2].wait()
        emit_faces(0, a, b, fluid[a, b])
        if e == count // 2 - 1 and len(hops) > 1:
            ag_relay(0, hops[1])
    send_faces(0)
    small[2].wait()

    for r in range(ROUNDS):
        last = r == ROUNDS - 1
        if r > 0:
            for i in range(max(len(hops), len(relays))):
                if i < len(relays):
                    rs_relay(r, relays[i])
                if i < len(hops):
                    ag_relay(r, hops[i])
        else:
            for k in relays[:half]:
                rs_relay(r, k)
            for s in hops[2:]:
                ag_relay(r, s)
        wall_in = dot(hot_t[...], csh[r].reshape(strip, NV * width)).astype(bf16)
        for d in range(4):
            when_do(gets[d], lambda d=d: face_copy(r, d).wait_recv())
        for e, (a, b) in enumerate(elements):
            x = new_fluid(r, a, b, wall_in)
            if last:
                fluid_out[a, b] = x
            else:
                fluid[a, b] = x
                emit_wall(a, b, x)
            if r == 0 and e == 1:
                for k in relays[half:]:
                    rs_relay(r, k)
            if e == 5:
                shell = shell_of(load_of(r))
                if last:
                    for s in range(SDOF):
                        shell_out[s] = shell[s]
                else:
                    gather_shell(r + 1, shell)
                    ag_start(r + 1)
        if not last:
            rs_start(r + 1)
            for a, b in elements:
                emit_faces(r + 1, a, b, fluid[a, b])
            send_faces(r + 1)

    for r in range(ROUNDS):
        ag_sent(r)
        rs_sent(r)
        faces_sent(r)


def per_device(n_span, n_chord, adj_rhs, diag_inv, face_jac, face_mask, wall_map, couple, shell_rhs, shell_inv):
    rows, cols, blk, width = adj_rhs.shape
    nodes = shell_rhs.shape[0]
    walls = rows * cols * NF
    strip = n_chord * nodes
    bf16 = jnp.bfloat16
    place = placement()
    vmem = pl.BlockSpec(memory_space=pltpu.VMEM)
    smem = pl.BlockSpec(memory_space=pltpu.SMEM)
    hbm = pl.BlockSpec(memory_space=pl.ANY)
    sem = pltpu.SemaphoreType.DMA
    fluid, shell = pl.pallas_call(
        functools.partial(kernel, n_span, n_chord),
        out_shape=(
            jax.ShapeDtypeStruct((rows, cols, blk, width), bf16),
            jax.ShapeDtypeStruct((SDOF, nodes, width), bf16),
        ),
        in_specs=[smem, smem, vmem, vmem, hbm, hbm, hbm, hbm, hbm, hbm],
        out_specs=(vmem, vmem),
        scratch_shapes=[
            pltpu.VMEM((SDOF, nodes, width), bf16),
            pltpu.VMEM((blk, 3 * FACE), bf16),
            pltpu.VMEM((FACE, blk), bf16),
            pltpu.VMEM((rows, cols, blk, width), bf16),
            pltpu.VMEM((rows, cols, blk, blk), bf16),
            pltpu.VMEM((rows, cols, 4, FACE, blk), bf16),
            pltpu.VMEM((rows, cols, blk, width), bf16),
            pltpu.VMEM((ROUNDS, rows, cols, FACE, width), bf16),
            pltpu.VMEM((ROUNDS, rows, cols, FACE, width), bf16),
            pltpu.VMEM((ROUNDS, cols, rows, FACE, width), bf16),
            pltpu.VMEM((ROUNDS, cols, rows, FACE, width), bf16),
            pltpu.VMEM((ROUNDS, 2, cols, FACE, width), bf16),
            pltpu.VMEM((ROUNDS, 2, rows, FACE, width), bf16),
            pltpu.VMEM((walls, NV * width), bf16),
            pltpu.VMEM((ROUNDS, n_chord, nodes, NV * width), jnp.float32),
            pltpu.VMEM((ROUNDS, 2, n_chord, nodes, NV * width), bf16),
            pltpu.VMEM((ROUNDS, 2, n_chord, nodes, NV * width), bf16),
            pltpu.VMEM((ROUNDS, n_chord, nodes, NV * width), bf16),
            pltpu.VMEM((strip, walls), bf16),
            pltpu.VMEM((walls, strip), bf16),
            sem((3,)),
            sem((3, rows * cols)),
            sem((ROUNDS, 2, n_chord)),
            sem((ROUNDS, 2, n_chord)),
            sem((ROUNDS, 2, n_chord)),
            sem((ROUNDS, 2, n_chord)),
            sem((ROUNDS, 4)),
            sem((ROUNDS, 4)),
        ],
        compiler_params=pltpu.CompilerParams(
            collective_id=0, has_side_effects=True, vmem_limit_bytes=60 * 2**20
        ),
    )(
        couple,
        face_mask,
        wall_map,
        shell_inv.transpose(1, 2, 0),
        shell_rhs.transpose(1, 0, 2),
        jnp.asarray(place, bf16),
        jnp.asarray(place[:, 2 * FACE :].T, bf16),
        adj_rhs,
        diag_inv,
        face_jac,
    )
    return fluid, shell.transpose(1, 0, 2)


def solution(mesh):
    return jax.shard_map(
        functools.partial(per_device, mesh.shape["span"], mesh.shape["chord"]),
        mesh=mesh,
        in_specs=(
            P("span", "chord", None, None),
            P("span", "chord", None, None),
            P("span", "chord", None, None, None),
            P("span", "chord", None),
            P("span", "chord", None),
            P(),
            P(("span", "chord"), None, None),
            P(("span", "chord"), None, None),
        ),
        out_specs=(P("span", "chord", None, None), P(("span", "chord"), None, None)),
        check_vma=False,
    )
```
